32 devices in a mesh: section: 2 (over y), expert: 8 (over z, core), dp: 2 (over x).
Axes of the slice: x: 2, y: 2, z: 4, core: 2. Of those that a mesh axis runs over, the one named last changes fastest.
Arguments:
- blocks: bfloat16 [2, 128, 7168], P('section', ('expert', 'dp')), may hold values from -6 to 6
- gains: float32 [2, 7168], P('section'), may hold values from 0.1 to 1.9
- w_gate: bfloat16 [2, 7168, 2048], P('section', 'dp', 'expert'), may hold values from -0.0625 to 0.0625
- w_up: bfloat16 [2, 7168, 2048], P('section', 'dp', 'expert'), may hold values from -0.0625 to 0.0625
- w_down: bfloat16 [2, 7168, 2048], P('section', 'dp', 'expert'), may hold values from -0.1875 to 0.1875
- expert_ids: int32 [2, 2, 128, 2], P('section', None, ('expert', 'dp')), may hold values from 0 to 1, all different within a row; in each aligned block of 8 rows (0 to 7, 8 to 15, ..., all dimensions but the last counted through in order) at most 8 rows name the same one
- combine: float32 [2, 2, 128, 2], P('section', None, ('expert', 'dp')), may hold values from 0.2 to 1
Outputs:
- finished: bfloat16 [2, 128, 7168], P('section', ('expert', 'dp'))
The draws below stay inside these ranges and needn't reach their ends.
Inputs may be any that keep to these rules, and one draw needn't show every extreme that they name: `expert_ids`: each token names 2 different experts; within the 8 tokens of one device (aligned blocks), no expert is named more than 8 times, a bound that some block reaches.
All inputs are finite; a program needn't handle non-finite values.
Results may differ from the reference program's by a relative error of at most 0.0073.
Values may be sent and summed in bfloat16 or wider, within the bound.
A program may use at most 64 MiB of HBM per device.

```python
import math
import jax
import jax.numpy as jnp
import numpy as np
from jax import lax

D = 7168
FF = 1024
TOP = 2
ROUNDS = 2
TOK_DEV = 8
EXPERTS = 2
CAP = 8
TOKENS = 128
N_SECTION = 2
N_EXPERT = 8


def level_of(own_key, dims, cuts, low, high):
    def one(position, parts):
        heights = jax.random.uniform(jax.random.fold_in(jax.random.fold_in(own_key, 6), position), (parts,), jnp.float32, low / len(cuts), high / len(cuts))
        return jnp.repeat(jnp.exp(heights), dims[position] // parts).reshape((-1,) + (1,) * (len(dims) - position - 1))

    level = one(*cuts[0])
    for cut in cuts[1:]:
        level = level * one(*cut)
    return level


def assign_block(rng, own, number, rows, amount, top, reach, slope):
    sequence = jax.random.permutation(rng, amount)
    crowded, common = load_shares(amount, rows * top, reach, slope, True), load_shares(amount, rows * top, reach, slope, False)
    places = jnp.arange(amount)

    def named(sizes, rotation):
        used = int((sizes > 0).sum())
        fixed = max(1, used // 4)
        shifted = fixed + (places - fixed + rotation * (used - fixed)) % max(1, amount - fixed)
        return jnp.zeros((amount,), jnp.int32).at[sequence[jnp.where(places < fixed, places, shifted)]].set(jnp.asarray(sizes, jnp.int32))

    sizes = jnp.where(number % 4 == 0, named(crowded, number // 4), named(common, number - number // 4 - 1))
    mixed = jax.random.permutation(jax.random.fold_in(own, 3), amount)
    giver, sink = mixed[0:amount // 2 * 2:2], mixed[1:amount // 2 * 2:2]
    slack = jnp.minimum(sizes[giver] - 1, reach - sizes[sink]) // 2
    slack = jnp.where((giver == sequence[0]) | (sink == sequence[0]) | (sizes[sink] == 0), 0, jnp.maximum(slack, 0))
    shifted = jax.random.randint(jax.random.fold_in(own, 4), (amount // 2,), 0, 1 << 20) % (slack + 1)
    sizes = sizes.at[giver].add(-shifted).at[sink].add(shifted)
    items = jnp.searchsorted(jnp.cumsum(sizes), jnp.arange(rows * top), side="right").astype(jnp.int32)
    grid = items.reshape(top, rows).T
    grid = grid[jax.random.permutation(jax.random.fold_in(own, 1), rows)]
    rotation = jax.random.randint(jax.random.fold_in(own, 2), (rows, 1), 0, top)
    return jnp.take_along_axis(grid, (jnp.arange(top)[None, :] + rotation) % top, axis=1)


def load_shares(count, total, bound, slope, full):
    portions = [(1 << 20) // math.isqrt(standing ** slope) + 1 for standing in range(1, count + 1)]
    largest = bound if full else min(bound, max(-(-total // count), total * portions[0] // sum(portions)))
    least = 1 if total - largest >= count - 1 else 0
    counts, surplus = [largest] + [least] * (count - 1), total - largest - least * (count - 1)
    while surplus > 0:
        candidates = [i for i in range(1, count) if counts[i] < largest] or [i for i in range(1, count) if counts[i] < bound]
        pool, budget = sum([portions[i] for i in candidates]), surplus
        for i in candidates:
            more = min(bound - counts[i], max(1, budget * portions[i] // pool), surplus)
            counts[i] = counts[i] + more
            surplus = surplus - more
    return np.array(counts)


def bell_draw(rng, dims, deviation, reach, split=(), held_as=jnp.bfloat16):
    result = jax.random.normal(rng, dims, jnp.float32) * deviation
    if len(split) > 0:
        result = level_of(rng, dims, split, -0.22, 0.18) * result
    return jnp.clip(result, min=-reach, max=reach).astype(held_as)


def setup_inputs(seed: int = 0) -> dict:
    key_of = jax.random.split(jax.random.key(seed), 8)
    blocks = bell_draw(key_of[0], (N_SECTION, TOKENS, D), 1.0, 6.0, ((0, 2), (1, 16)))
    gains = jnp.clip(1.0 + 0.18 * jax.random.normal(key_of[1], (N_SECTION, D), jnp.float32), 0.1, 1.9)
    w_gate = bell_draw(key_of[2], (N_SECTION, D, EXPERTS * FF), D ** -0.5, 0.0625, ((0, 2), (1, 2), (2, 8)))
    w_up = bell_draw(key_of[3], (N_SECTION, D, EXPERTS * FF), D ** -0.5, 0.0625, ((0, 2), (1, 2), (2, 8)))
    w_down = bell_draw(key_of[4], (N_SECTION, D, EXPERTS * FF), FF ** -0.5, 0.1875, ((0, 2), (1, 2), (2, 8)))
    expert_ids_keys = jax.random.split(jax.random.fold_in(key_of[5], 1), N_SECTION * ROUNDS * TOKENS // TOK_DEV)
    expert_ids_turns = jax.random.permutation(jax.random.fold_in(key_of[5], 3), N_SECTION * ROUNDS * TOKENS // TOK_DEV)
    expert_ids = jax.vmap(lambda own, number: assign_block(jax.random.fold_in(key_of[5], 2), own, number, TOK_DEV, EXPERTS, TOP, CAP, 2))(expert_ids_keys, expert_ids_turns).reshape((N_SECTION, ROUNDS, TOKENS, TOP))
    combine = jnp.clip(0.2 + 0.8 * jax.random.uniform(key_of[6], (N_SECTION, ROUNDS, TOKENS, TOP), jnp.float32) ** level_of(key_of[6], (N_SECTION, ROUNDS, TOKENS, TOP), ((0, 2), (2, 16)), -0.2, 0.2), 0.2, 1.0)
    return dict(blocks=blocks, gains=gains, w_gate=w_gate, w_up=w_up, w_down=w_down, expert_ids=expert_ids, combine=combine)


def layer_step(stream, gain_row, gate_w, up_w, down_w, route, mixing):
    widened = stream.astype(jnp.float32)
    inv_rms = lax.rsqrt(lax.optimization_barrier(jnp.mean(widened * widened, axis=1, keepdims=True)) + 1e-06)
    normed = (widened * inv_rms * gain_row[None, :]).astype(jnp.bfloat16)
    sources = TOKENS // TOK_DEV
    span = N_EXPERT // EXPERTS
    slice_width = FF // span
    grouped = route.reshape(sources, TOK_DEV * TOP)
    chosen = (grouped[:, :, None] == jnp.arange(EXPERTS, dtype=jnp.int32)[None, None, :]).astype(jnp.int32)
    running = jnp.cumsum(chosen, axis=1)
    slot_of = lax.optimization_barrier(jnp.sum(chosen * (running - 1), axis=2)).astype(jnp.int32)
    row_of = (jnp.arange(sources, dtype=jnp.int32)[:, None] * CAP + slot_of).reshape(-1).astype(jnp.int32)
    flat_ids = route.reshape(-1).astype(jnp.int32)
    copies = jnp.repeat(normed, TOP, axis=0)
    buffer = jnp.zeros((EXPERTS, sources * CAP, D), jnp.bfloat16).at[flat_ids, row_of].set(copies)
    gate_each = gate_w.reshape(D, EXPERTS, FF).transpose(1, 0, 2)
    up_each = up_w.reshape(D, EXPERTS, FF).transpose(1, 0, 2)
    down_each = down_w.reshape(D, EXPERTS, FF).transpose(1, 0, 2)

    def one_expert(operands):
        rows_in, gate_full, up_full, down_full = operands
        gate_act = jnp.dot(rows_in, gate_full, preferred_element_type=jnp.float32)
        upward = jnp.dot(rows_in, up_full, preferred_element_type=jnp.float32)
        hidden = (jax.nn.silu(gate_act) * upward).astype(jnp.bfloat16)
        hidden_blocks = hidden.astype(jnp.float32).reshape(rows_in.shape[0], span, slice_width)
        down_blocks = down_full.astype(jnp.float32).reshape(D, span, slice_width)
        pieces = jnp.einsum('rsf,dsf->srd', hidden_blocks, down_blocks)
        rounded = lax.optimization_barrier(pieces.astype(jnp.bfloat16))
        return lax.optimization_barrier(jnp.sum(rounded.astype(jnp.float32), axis=0)).astype(jnp.bfloat16)
    outputs = lax.map(one_expert, (buffer, gate_each, up_each, down_each))
    picked = outputs[flat_ids, row_of].reshape(TOKENS, TOP, D)
    mixed_sum = lax.optimization_barrier(jnp.sum(mixing[:, :, None] * picked.astype(jnp.float32), axis=1))
    return (widened + mixed_sum).astype(jnp.bfloat16)

def reference(blocks, gains, w_gate, w_up, w_down, expert_ids, combine):
    finished = []
    for section_pos in range(N_SECTION):
        start_block = (section_pos - ROUNDS + 1) % N_SECTION
        stream = blocks[start_block]
        for layer_turn in range(ROUNDS):
            layer_index = (start_block + layer_turn) % N_SECTION
            stream = layer_step(stream, gains[layer_index], w_gate[layer_index], w_up[layer_index], w_down[layer_index], expert_ids[layer_index, layer_turn], combine[layer_index, layer_turn])
        finished.append(stream)
    return jnp.stack(finished)
```

```python
from functools import partial

import jax
import jax.numpy as jnp
from jax import lax
from jax.experimental import pallas as pl
from jax.experimental.pallas import tpu as pltpu
from jax.sharding import PartitionSpec as P

F32 = jnp.float32
BF16 = jnp.bfloat16
MESH = pl.DeviceIdType.MESH


def folded(rows):
    half = rows.shape[1] // 2
    return jnp.concatenate([rows[:, :half], rows[:, half:]], axis=0).astype(BF16)


def unfolded(rows):
    wide = rows.astype(F32)
    count = rows.shape[0] // 2
    return jnp.concatenate([wide[:count], wide[count:]], axis=1)


def kernel(
    owners, sections, turns,
    x_ref, gain_ref, gate_hbm, up_hbm, down_hbm, ids_ref, mix_ref,
    out_ref,
    gate_w, up_w, down_w,
    coef, coef_in, half_out, half_in, rows_all, act_out, act_in,
    part, part_in, chip, chip_in, mixed_out, mixed_in, hop_out, hop_in,
    w_sem, ssem, rsem,
):
    experts = max(2, owners // 8)
    span = owners // experts
    pairs = owners // 2
    sec = lax.axis_index("section")
    own = lax.axis_index("expert")
    p = lax.axis_index("dp")
    z = own // 2
    c = lax.rem(own, 2)
    half = gate_w.shape[0]
    tok = x_ref.shape[1]

    def z_of(d):
        return lax.rem(z + d, pairs)

    sibling = {"expert": 2 * z + 1 - c}
    partner = {"dp": 1 - p}
    onward = {"section": lax.rem(sec + 1, sections)}
    backward = {"section": lax.rem(sec + sections - 1, sections)}

    def peer(d):
        return {"expert": 2 * z_of(d) + c}

    barrier = pltpu.get_barrier_semaphore()
    greeted = [sibling, partner, onward] + [peer(d) for d in range(1, pairs)]
    if sections > 2:
        greeted.append(backward)
    for who in greeted:
        pl.semaphore_signal(barrier, inc=1, device_id=who, device_id_type=MESH)

    loads = [
        pltpu.make_async_copy(src, dst, w_sem.at[i])
        for i, (src, dst) in enumerate(((gate_hbm.at[0], gate_w), (up_hbm.at[0], up_w), (down_hbm.at[0], down_w)))
    ]
    for load in loads:
        load.start()

    counter = [0]

    def send(src, dst, who):
        i = counter[0]
        counter[0] += 1
        copy = pltpu.make_async_remote_copy(
            src_ref=src, dst_ref=dst, send_sem=ssem.at[i], recv_sem=rsem.at[i],
            device_id=who, device_id_type=MESH,
        )
        copy.start()
        return copy

    first = p == 0
    lane = lax.broadcasted_iota(jnp.int32, (tok, 128), 1)
    for r in range(turns):
        ids = ids_ref[0, r]
        mix = mix_ref[0, r]
        table = jnp.zeros((tok, 128), F32)
        for k in range(ids.shape[1]):
            table += jnp.where(lane == ids[:, k : k + 1], mix[:, k : k + 1], 0.0)
        coef[r] = table

    lane16 = lax.broadcasted_iota(jnp.int32, (2 * tok, 128), 1)
    waiting = []
    gain = gain_ref[...]
    stream = x_ref[0].astype(F32)
    for r in range(turns):
        inv = lax.rsqrt(jnp.mean(stream * stream, axis=1, keepdims=True) + 1e-06)
        normed = stream * inv * gain
        lo, hi = normed[:, :half], normed[:, half:]
        keep = jnp.where(first, lo, hi)
        half_out[r] = folded(jnp.where(first, hi, lo))
        if r == 0:
            pl.semaphore_wait(barrier, len(greeted))
            coef_copy = send(coef, coef_in, partner)
            waiting.append(coef_copy)
        copy = send(half_out.at[r], half_in.at[r], partner)
        copy.wait_recv()
        waiting.append(copy)
        other = unfolded(half_in[r])
        block = jnp.concatenate([jnp.where(first, keep, other), jnp.where(first, other, keep)], axis=0)
        rows_all[r, c, z] = block.astype(BF16)

        mine = rows_all.at[r, c, z]
        around = [send(mine, mine, peer(d)) for d in range(1, pairs)]
        across = [send(mine, mine, sibling)]
        for d in range(1, pairs):
            around[d - 1].wait_recv()
            came = rows_all.at[r, c, z_of(pairs - d)]
            across.append(send(came, came, sibling))
        for copy in across:
            copy.wait_recv()
        waiting += around + across

        if r == 0:
            loads[0].wait()
            loads[1].wait()
        rows = rows_all[r].reshape(owners * 2 * tok, half)
        gate = jnp.dot(rows, gate_w[...], preferred_element_type=F32)
        up = jnp.dot(rows, up_w[...], preferred_element_type=F32)
        act_out[r, 0] = gate.astype(BF16)
        act_out[r, 1] = up.astype(BF16)
        copy = send(act_out.at[r], act_in.at[r], partner)
        copy.wait_recv()
        waiting.append(copy)
        gate += act_in[r, 0].astype(F32)
        up += act_in[r, 1].astype(F32)
        hidden = (gate / (1.0 + jnp.exp(-gate)) * up).astype(BF16)

        if r == 0:
            loads[2].wait()
        partial_out = lax.dot_general(
            hidden, down_w[...], (((1,), (1,)), ((), ())), preferred_element_type=F32
        )
        part[r] = partial_out.astype(BF16).reshape(2, pairs, 2 * tok, half)
        copy = send(part.at[r, 1 - c], part_in.at[r], sibling)
        copy.wait_recv()
        waiting.append(copy)

        around = []
        for d in range(1, pairs):
            there = z_of(d)
            chip[r, d] = (part[r, c, there].astype(F32) + part_in[r, there].astype(F32)).astype(BF16)
            around.append(send(chip.at[r, d], chip_in.at[r, d], peer(d)))
        waiting += around

        if r == 0:
            coef_copy.wait_recv()
        mine, theirs = coef[r], coef_in[r]
        table = jnp.concatenate([jnp.where(first, mine, theirs), jnp.where(first, theirs, mine)], axis=0)

        def weight(source):
            return jnp.sum(jnp.where(lane16 == source * 2 // span, table, 0.0), axis=1, keepdims=True)

        total = weight(z) * (part[r, c, z].astype(F32) + part_in[r, z].astype(F32))
        for d in range(1, pairs):
            around[d - 1].wait_recv()
            total += weight(z_of(pairs - d)) * chip_in[r, d].astype(F32)
        keep = jnp.where(first, total[:tok], total[tok:])
        mixed_out[r] = folded(jnp.where(first, total[tok:], total[:tok]))
        copy = send(mixed_out.at[r], mixed_in.at[r], partner)
        copy.wait_recv()
        waiting.append(copy)
        other = unfolded(mixed_in[r])
        stream = stream + jnp.concatenate(
            [jnp.where(first, keep, other), jnp.where(first, other, keep)], axis=1
        )
        if r < turns - 1:
            hop_out[r] = folded(stream)
            copy = send(hop_out.at[r], hop_in.at[r], onward)
            copy.wait_recv()
            waiting.append(copy)
            stream = unfolded(hop_in[r])
        else:
            out_ref[0] = stream.astype(BF16)
    for copy in waiting:
        copy.wait_send()


def on_device(blocks, gains, w_gate, w_up, w_down, expert_ids, combine):
    owners = lax.axis_size("expert")
    sections = lax.axis_size("section")
    turns = expert_ids.shape[1]
    tok = blocks.shape[1]
    width = blocks.shape[2]
    half, cols = w_gate.shape[1:]
    pairs = owners // 2
    rows = 2 * tok
    sends = 1 + turns * (1 + (pairs - 1) + pairs + 1 + 1 + (pairs - 1) + 1) + turns - 1
    vmem = pl.BlockSpec(memory_space=pltpu.VMEM)
    hbm = pl.BlockSpec(memory_space=pl.ANY)
    return pl.pallas_call(
        partial(kernel, owners, sections, turns),
        out_shape=jax.ShapeDtypeStruct(blocks.shape, BF16),
        in_specs=[vmem, vmem, hbm, hbm, hbm, vmem, vmem],
        out_specs=vmem,
        scratch_shapes=[
            pltpu.VMEM((half, cols), BF16),
            pltpu.VMEM((half, cols), BF16),
            pltpu.VMEM((half, cols), BF16),
            pltpu.VMEM((turns, tok, 128), F32),
            pltpu.VMEM((turns, tok, 128), F32),
            pltpu.VMEM((turns, rows, half // 2), BF16),
            pltpu.VMEM((turns, rows, half // 2), BF16),
            pltpu.VMEM((turns, 2, pairs, rows, half), BF16),
            pltpu.VMEM((turns, 2, owners * rows, cols), BF16),
            pltpu.VMEM((turns, 2, owners * rows, cols), BF16),
            pltpu.VMEM((turns, 2, pairs, rows, half), BF16),
            pltpu.VMEM((turns, pairs, rows, half), BF16),
            pltpu.VMEM((turns, pairs, rows, half), BF16),
            pltpu.VMEM((turns, pairs, rows, half), BF16),
            pltpu.VMEM((turns, rows, half // 2), BF16),
            pltpu.VMEM((turns, rows, half // 2), BF16),
            pltpu.VMEM((max(1, turns - 1), rows, width // 2), BF16),
            pltpu.VMEM((max(1, turns - 1), rows, width // 2), BF16),
            pltpu.SemaphoreType.DMA((3,)),
            pltpu.SemaphoreType.DMA((sends,)),
            pltpu.SemaphoreType.DMA((sends,)),
        ],
        compiler_params=pltpu.CompilerParams(
            collective_id=0, has_side_effects=True, vmem_limit_bytes=56 * 2**20
        ),
    )(blocks, gains, w_gate, w_up, w_down, expert_ids, combine)


def solution(mesh):
    in_specs = (
        P("section", ("expert", "dp"), None),
        P("section", None),
        P("section", "dp", "expert"),
        P("section", "dp", "expert"),
        P("section", "dp", "expert"),
        P("section", None, ("expert", "dp"), None),
        P("section", None, ("expert", "dp"), None),
    )
    out_specs = P("section", ("expert", "dp"), None)
    return jax.shard_map(
        on_device, mesh=mesh, in_specs=in_specs, out_specs=out_specs, check_vma=False
    )
```

```python
from functools import partial

import jax
import jax.numpy as jnp
from jax import lax
from jax.experimental import pallas as pl
from jax.experimental.pallas import tpu as pltpu
from jax.sharding import PartitionSpec as P

F32 = jnp.float32
BF16 = jnp.bfloat16
MESH = pl.DeviceIdType.MESH


def folded(rows):
    half = rows.shape[1] // 2
    return jnp.concatenate([rows[:, :half], rows[:, half:]], axis=0).astype(BF16)


def unfolded(rows):
    wide = rows.astype(F32)
    count = rows.shape[0] // 2
    return jnp.concatenate([wide[:count], wide[count:]], axis=1)


def kernel(
    owners, sections, turns,
    x_ref, gain_ref, gate_hbm, up_hbm, down_hbm, ids_ref, mix_ref,
    out_ref,
    gate_w, up_w, down_w,
    coef, coef_in, half_out, half_in, rows_all, act_out, act_in,
    part, part_in, chip, chip_in, hop_out, hop_in, square_out, square_in, last_out, last_in,
    w_sem, line_s, line_r, pair_s, pair_r, act_s, act_r, part_s, part_r, back_s, back_r, ssem, rsem,
):
    experts = max(2, owners // 8)
    span = owners // experts
    pairs = owners // 2
    sec = lax.axis_index("section")
    own = lax.axis_index("expert")
    p = lax.axis_index("dp")
    z = own // 2
    c = lax.rem(own, 2)
    half = gate_w.shape[0]
    tok = x_ref.shape[1]
    width = x_ref.shape[2]
    ahead, behind = lax.rem(sec + 1, sections), lax.rem(sec + sections - 1, sections)

    sibling = {"expert": 2 * z + 1 - c}
    partner = {"dp": 1 - p}
    onward = {"section": ahead}
    slanted = {"section": ahead, "dp": 1 - p}

    def peer(at):
        return {"expert": 2 * at + c}

    barrier = pltpu.get_barrier_semaphore()
    greeted = [sibling, partner, onward, slanted]
    greeted += [peer(lax.rem(z + d, pairs)) for d in range(1, pairs)]
    if sections > 2:
        greeted += [{"section": behind}, {"section": behind, "dp": 1 - p}]
    for who in greeted:
        pl.semaphore_signal(barrier, inc=1, device_id=who, device_id_type=MESH)

    loads = [
        pltpu.make_async_copy(src, dst, w_sem.at[i])
        for i, (src, dst) in enumerate(((gate_hbm.at[0], gate_w), (up_hbm.at[0], up_w), (down_hbm.at[0], down_w)))
    ]
    for load in loads:
        load.start()

    def remote(src, dst, s, r, who):
        return pltpu.make_async_remote_copy(
            src_ref=src, dst_ref=dst, send_sem=s, recv_sem=r, device_id=who, device_id_type=MESH
        )

    waiting = []
    guarded = []
    counter = [0]

    def start(copy):
        copy.start()
        waiting.append(copy)
        return copy

    def start_if(flag, copy):
        @pl.when(flag)
        def _():
            copy.start()

        guarded.append((flag, copy))

    def send(src, dst, who):
        i = counter[0]
        counter[0] += 1
        return start(remote(src, dst, ssem.at[i], rsem.at[i], who))

    short = jnp.minimum(z, pairs - 1 - z)
    low = 2 * z < pairs - 1
    order = [z]
    for j in range(1, pairs):
        d = (j + 1) // 2
        near = jnp.where(low, -d, d) if j % 2 == 1 else jnp.where(low, d, -d)
        far = jnp.where(low, j - short, short - j)
        order.append(z + jnp.where(j <= 2 * short, near, far))

    first = p == 0
    even = c == 0
    lane = lax.broadcasted_iota(jnp.int32, (tok, 128), 1)
    for r in range(turns):
        ids = ids_ref[0, r]
        mix = mix_ref[0, r]
        table = jnp.zeros((tok, 128), F32)
        for k in range(ids.shape[1]):
            table += jnp.where(lane == ids[:, k : k + 1], mix[:, k : k + 1], 0.0)
        coef[r] = table

    def both(mine, theirs):
        return jnp.concatenate([jnp.where(first, mine, theirs), jnp.where(first, theirs, mine)], axis=0)

    whole = x_ref[0].astype(F32)
    lo, hi = whole[:, :half], whole[:, half:]
    half_out[...] = folded(jnp.where(first, hi, lo))
    squares = jnp.sum(whole * whole, axis=1, keepdims=True)
    coef[turns] = jnp.broadcast_to(squares, (tok, 128))
    pl.semaphore_wait(barrier, len(greeted))
    half_copy = send(half_out, half_in, partner)
    coef_copy = send(coef, coef_in, partner)
    gain = jnp.where(first, gain_ref[:, :half], gain_ref[:, half:])
    half_copy.wait_recv()
    coef_copy.wait_recv()
    stream = both(jnp.where(first, lo, hi), unfolded(half_in[...]))
    squares = both(coef[turns], coef_in[turns])[:, :1]
    lane16 = lax.broadcasted_iota(jnp.int32, (2 * tok, 128), 1)

    for r in range(turns):
        inv = lax.rsqrt(squares / width + 1e-06)
        rows_all[r, z, c] = (stream * inv * gain).astype(BF16)
        mine = rows_all.at[r, z, c]
        left = remote(mine, mine, line_s.at[r, 0], line_r.at[r, z], peer(jnp.maximum(z - 1, 0)))
        right = remote(mine, mine, line_s.at[r, pairs], line_r.at[r, z], peer(jnp.minimum(z + 1, pairs - 1)))
        start_if(z > 0, left)
        start_if(z < pairs - 1, right)
        table = both(coef[r], coef_in[r])

        def weight(source):
            return jnp.sum(jnp.where(lane16 == source * 2 // span, table, 0.0), axis=1, keepdims=True)

        acts, parts, backs, kept = {}, {}, {}, {}

        def multiply(j):
            b = order[j]
            block = rows_all.at[r, b, c]
            if j > 0:
                remote(block, block, line_s.at[r, j], line_r.at[r, b], sibling).wait_recv()
                to = jnp.where(b < z, z + 1, z - 1)
                inside = (to >= 0) & (to < pairs)
                to = jnp.clip(to, 0, pairs - 1)
                start_if(inside, remote(block, block, line_s.at[r, j], line_r.at[r, b], peer(to)))
            start(remote(block, block, pair_s.at[r, j], pair_r.at[r, j], sibling)).wait_recv()
            if r == 0 and j == 0:
                loads[0].wait()
                loads[1].wait()
            rows = rows_all[r, b].reshape(4 * tok, half)
            gate = jnp.dot(rows, gate_w[...], preferred_element_type=F32)
            up = jnp.dot(rows, up_w[...], preferred_element_type=F32)
            act_out[r, j, 0] = gate.astype(BF16)
            act_out[r, j, 1] = up.astype(BF16)
            copy = start(remote(act_out.at[r, j], act_in.at[r, j], act_s.at[r, j], act_r.at[r, j], partner))
            acts[j] = (gate, up, copy)

        def project(j):
            gate, up, copy = acts.pop(j)
            copy.wait_recv()
            gate = gate + act_in[r, j, 0].astype(F32)
            up = up + act_in[r, j, 1].astype(F32)
            hidden = (gate / (1.0 + jnp.exp(-gate)) * up).astype(BF16)
            if r == 0 and j == 0:
                loads[2].wait()
            part[r, j] = lax.dot_general(
                hidden, down_w[...], (((1,), (1,)), ((), ())), preferred_element_type=F32
            ).astype(BF16).reshape(2, 2 * tok, half)
            parts[j] = start(
                remote(part.at[r, j, 1 - c], part_in.at[r, j], part_s.at[r, j], part_r.at[r, j], sibling)
            )

        def give_back(j):
            parts.pop(j).wait_recv()
            summed = part[r, j, c].astype(F32) + part_in[r, j].astype(F32)
            if j == 0:
                kept[0] = weight(z) * summed
            else:
                chip[r, j] = summed.astype(BF16)
                start(remote(chip.at[r, j], chip_in.at[r, z], back_s.at[r, j], back_r.at[r, z], peer(order[j])))

        for j in range(pairs + 2):
            if j < pairs:
                multiply(j)
            if 0 <= j - 1 < pairs:
                project(j - 1)
            if 0 <= j - 2 < pairs:
                give_back(j - 2)

        total = kept[0]
        for j in range(1, pairs):
            b = order[j]
            slot = chip_in.at[r, b]
            remote(slot, slot, back_s.at[r, j], back_r.at[r, b], sibling).wait_recv()
            total += weight(b) * chip_in[r, b].astype(F32)
        after = (stream + total).astype(BF16)
        stream = after.astype(F32)
        if r < turns - 1:
            hop_out[r] = after
            hop = send(hop_out.at[r], hop_in.at[r], onward)
            squares = jnp.sum(stream * stream, axis=1, keepdims=True)
            square_out[r] = jnp.broadcast_to(squares, (2 * tok, 128))
            square = send(square_out.at[r], square_in.at[r], slanted)
            hop.wait_recv()
            stream = hop_in[r].astype(F32)
            squares = jnp.sum(stream * stream, axis=1, keepdims=True)
            square.wait_recv()
            squares += square_in[r][:, :1]
        else:
            keep = jnp.where(first, stream[:tok], stream[tok:])
            last_out[...] = folded(jnp.where(first, stream[tok:], stream[:tok]))
            send(last_out, last_in, partner).wait_recv()
            other = unfolded(last_in[...])
            out_ref[0] = jnp.concatenate(
                [jnp.where(first, keep, other), jnp.where(first, other, keep)], axis=1
            ).astype(BF16)
    for copy in waiting:
        copy.wait_send()
    for flag, copy in guarded:
        pl.when(flag)(copy.wait_send)


def on_device(blocks, gains, w_gate, w_up, w_down, expert_ids, combine):
    owners = lax.axis_size("expert")
    sections = lax.axis_size("section")
    turns = expert_ids.shape[1]
    tok = blocks.shape[1]
    half, cols = w_gate.shape[1:]
    pairs = owners // 2
    rows = 2 * tok
    hops = max(1, turns - 1)
    sends = 3 + 2 * hops
    vmem = pl.BlockSpec(memory_space=pltpu.VMEM)
    hbm = pl.BlockSpec(memory_space=pl.ANY)
    return pl.pallas_call(
        partial(kernel, owners, sections, turns),
        out_shape=jax.ShapeDtypeStruct(blocks.shape, BF16),
        in_specs=[vmem, vmem, hbm, hbm, hbm, vmem, vmem],
        out_specs=vmem,
        scratch_shapes=[
            pltpu.VMEM((half, cols), BF16),
            pltpu.VMEM((half, cols), BF16),
            pltpu.VMEM((half, cols), BF16),
            pltpu.VMEM((turns + 1, tok, 128), F32),
            pltpu.VMEM((turns + 1, tok, 128), F32),
            pltpu.VMEM((rows, half // 2), BF16),
            pltpu.VMEM((rows, half // 2), BF16),
            pltpu.VMEM((turns, pairs, 2, rows, half), BF16),
            pltpu.VMEM((turns, pairs, 2, 2 * rows, cols), BF16),
            pltpu.VMEM((turns, pairs, 2, 2 * rows, cols), BF16),
            pltpu.VMEM((turns, pairs, 2, rows, half), BF16),
            pltpu.VMEM((turns, pairs, rows, half), BF16),
            pltpu.VMEM((turns, pairs, rows, half), BF16),
            pltpu.VMEM((turns, pairs, rows, half), BF16),
            pltpu.VMEM((hops, rows, half), BF16),
            pltpu.VMEM((hops, rows, half), BF16),
            pltpu.VMEM((hops, rows, 128), F32),
            pltpu.VMEM((hops, rows, 128), F32),
            pltpu.VMEM((rows, half // 2), BF16),
            pltpu.VMEM((rows, half // 2), BF16),
            pltpu.SemaphoreType.DMA((3,)),
            pltpu.SemaphoreType.DMA((turns, pairs + 1)),
        ]
        + [pltpu.SemaphoreType.DMA((turns, pairs))] * 9
        + [pltpu.SemaphoreType.DMA((sends,))] * 2,
        compiler_params=pltpu.CompilerParams(
            collective_id=0, has_side_effects=True, vmem_limit_bytes=56 * 2**20
        ),
    )(blocks, gains, w_gate, w_up, w_down, expert_ids, combine)


def solution(mesh):
    in_specs = (
        P("section", ("expert", "dp"), None),
        P("section", None),
        P("section", "dp", "expert"),
        P("section", "dp", "expert"),
        P("section", "dp", "expert"),
        P("section", None, ("expert", "dp"), None),
        P("section", None, ("expert", "dp"), None),
    )
    out_specs = P("section", ("expert", "dp"), None)
    return jax.shard_map(
        on_device, mesh=mesh, in_specs=in_specs, out_specs=out_specs, check_vma=False
    )
```
